32 devices in a mesh: quarter: 4 (over y, x), row: 2 (over core), col: 4 (over z).
Axes of the slice: x: 2, y: 2, z: 4, core: 2. Of those that a mesh axis runs over, the one named last changes fastest.
Arguments:
- grad: bfloat16 [4, 4096, 4096], P('quarter', 'row', 'col'), may hold values from -6 to 6
- left_root: bfloat16 [4096, 4096], P('row', 'col'), may hold values from -1 to 3, as said below
- right_root: bfloat16 [4, 4096, 4096], P('quarter', 'row', 'col'), may hold values from -1 to 3, as said below
- momentum: float32 [4, 4096, 4096], P('quarter', 'row', 'col'), may hold values from -6 to 6
- weights: bfloat16 [4, 4096, 4096], P('quarter', 'row', 'col'), may hold values from -6 to 6
Outputs:
- momentum_new: float32 [4, 4096, 4096], P('quarter', 'row', 'col')
- new_weights: bfloat16 [4, 4096, 4096], P(None, ('row', 'quarter'), 'col')
The draws below stay inside these ranges and needn't reach their ends.
Inputs may be any that keep to these rules, and one draw needn't show every extreme that they name: `left_root`: symmetric. `right_root`: each block symmetric.
All inputs are finite; a program needn't handle non-finite values.
Results may differ from the reference program's by a relative error of at most 0.001.
Values may be sent and summed in bfloat16 or wider, within the bound.
A program may use at most 128 MiB of HBM per device.

```python
import math
import jax
import jax.numpy as jnp

ROWS = 4096
COLS = 4096
QUARTERS = 4


def root_factor(key, order):
    first, second = jax.random.split(key)
    noise = jax.random.normal(first, (order, order), jnp.float32)
    symmetric = (noise + noise.T) * (0.35 / math.sqrt(order))
    diagonal = jnp.exp(jax.random.uniform(second, (order,), jnp.float32, math.log(0.5), math.log(2.0)))
    return symmetric + jnp.diag(diagonal)


def draw_left_root(key, part):
    return root_factor(jax.random.fold_in(key, 11), ROWS).astype(jnp.bfloat16)


def draw_right_root(key, part):
    keys = jax.random.split(jax.random.fold_in(key, 23), QUARTERS)
    blocks = [root_factor(keys[number], COLS) for number in range(QUARTERS)]
    return jnp.stack(blocks).astype(jnp.bfloat16)


def block_levels(own_key, extent, shards, least, largest):
    loudness, own = 1.0, jax.random.fold_in(own_key, 6)
    for axis_at, blocks in shards:
        steps = jnp.exp(jax.random.uniform(jax.random.fold_in(own, axis_at), (blocks,), jnp.float32, least / len(shards), largest / len(shards)))
        loudness = loudness * jnp.repeat(steps, extent[axis_at] // blocks).reshape([-1 if axis == axis_at else 1 for axis in range(len(extent))])
    return loudness


def centred(rng, dims, deviation, most, shards=(), held_as=jnp.bfloat16):
    factor_of = block_levels(rng, dims, shards, -0.22, 0.18) if shards else 1.0
    entries = jax.random.normal(rng, dims, jnp.float32) * deviation * factor_of
    return jnp.minimum(jnp.maximum(entries, -most), most).astype(held_as)


def setup_inputs(seed: int = 0) -> dict:
    splits = jax.random.split(jax.random.key(seed), 6)
    return {
        "grad": centred(splits[0], (QUARTERS, ROWS, COLS), 1.0, 6.0, ((0, 4), (1, 2), (2, 4))),
        "left_root": draw_left_root(jax.random.fold_in(splits[5], 71), 0),
        "right_root": draw_right_root(jax.random.fold_in(splits[5], 71), 0),
        "momentum": centred(splits[3], (QUARTERS, ROWS, COLS), 1.0, 6.0, ((0, 4), (1, 2), (2, 4)), jnp.float32),
        "weights": centred(splits[4], (QUARTERS, ROWS, COLS), 1.0, 6.0, ((0, 4), (1, 2), (2, 4))),
    }


decay_rate = 0.9
step_rate = 0.1


def reference(grad, left_root, right_root, momentum, weights):
    moments = []
    updates = []
    for quarter in range(QUARTERS):
        mixed = jnp.dot(grad[quarter], right_root[quarter], preferred_element_type=jnp.float32).astype(jnp.bfloat16)
        product = jnp.dot(left_root, mixed, preferred_element_type=jnp.float32)
        renewed = decay_rate * momentum[quarter] + (1.0 - decay_rate) * product
        updated = (weights[quarter].astype(jnp.float32) - step_rate * renewed).astype(jnp.bfloat16)
        moments.append(renewed)
        updates.append(updated)
    return jnp.stack(moments), jnp.stack(updates)
```

```python
import functools

import jax
import jax.numpy as jnp
from jax import lax
from jax.experimental import pallas as pl
from jax.experimental.pallas import tpu as pltpu
from jax.sharding import PartitionSpec as P

decay_rate = 0.9
step_rate = 0.1

CHUNKS = 8
PARTS = 2


def remote(src, dst, send, recv, device):
    return pltpu.make_async_remote_copy(
        src_ref=src, dst_ref=dst, send_sem=send, recv_sem=recv,
        device_id=device, device_id_type=pl.DeviceIdType.MESH,
    )


def kernel(
    grad, left, right, mom, wts, out_m, out_w,
    lbuf, gbuf, rbuf, mix, stage, mslot,
    lz_send, lz_recv, lxy_send, lxy_recv, local, own_send, own_recv,
    near_send, near_recv, far_send, far_recv,
    ms_send, ms_recv, me_send, me_recv,
    a_send, a_recv, m_in, m_out,
):
    rows, cols = left.shape
    lane = rows // 4
    step = rows // CHUNKS
    q, r, c = lax.axis_index("quarter"), lax.axis_index("row"), lax.axis_index("col")
    peers = [3 - q, q + 1 - 2 * (q % 2), (q + 2) % 4]
    twin = (q, 1 - r, c)
    inner = (c + 1) // 2 % 2 == 1
    outer = (c + 1) // 2 % 2 == 0
    before, after = (q, r, c - 1), (q, r, c + 1)
    low = c // 2 == 0
    pair = c + 1 - 2 * (c % 2)
    other = 3 - c
    mine = pl.ds(pl.multiple_of(q * lane, lane), lane)

    barrier = pltpu.get_barrier_semaphore()
    for p in peers:
        pl.semaphore_signal(barrier, inc=1, device_id=(p, r, c), device_id_type=pl.DeviceIdType.MESH)
    pl.semaphore_signal(barrier, inc=1, device_id=twin, device_id_type=pl.DeviceIdType.MESH)

    @pl.when(c > 0)
    def _():
        pl.semaphore_signal(barrier, inc=1, device_id=before, device_id_type=pl.DeviceIdType.MESH)

    @pl.when(c < 3)
    def _():
        pl.semaphore_signal(barrier, inc=1, device_id=after, device_id_type=pl.DeviceIdType.MESH)

    @pl.when(inner)
    def _():
        pl.semaphore_wait(barrier, 6)

    @pl.when(outer)
    def _():
        pl.semaphore_wait(barrier, 5)

    def lz(k, way, src):
        return remote(src, lbuf.at[k, mine], lz_send.at[k * 2 + way], lz_recv.at[k], after if way else before)

    def lxy(k, t):
        piece = lbuf.at[k, mine]
        return remote(piece, piece, lxy_send.at[k * 3 + t], lxy_recv.at[k * 4 + q], (peers[t], r, c))

    @pl.when(c < 3)
    def _():
        lz(c, 1, left.at[mine]).start()

    @pl.when(c > 0)
    def _():
        lz(c, 0, left.at[mine]).start()

    copy_l = pltpu.make_async_copy(left, lbuf.at[c], local.at[0])
    copy_l.start()

    def g_own():
        return remote(grad.at[0], gbuf.at[c], own_send.at[0], own_recv.at[0], (q, r, other))

    def r_own():
        half = rbuf.at[0, pl.ds(pl.multiple_of(r * rows, rows), rows)]
        return remote(right.at[0], half, own_send.at[1], own_recv.at[1], twin)

    def r_end():
        half = rbuf.at[1, pl.ds(pl.multiple_of(r * rows, rows), rows)]
        return remote(right.at[0], half, own_send.at[2], own_recv.at[2], (q, r, pair))

    def r_twin():
        half = rbuf.at[1, pl.ds(pl.multiple_of(r * rows, rows), rows)]
        return remote(half, half, own_send.at[3], own_recv.at[3], twin)

    copy_g = pltpu.make_async_copy(grad.at[0], gbuf.at[c], local.at[1])
    copy_r = pltpu.make_async_copy(
        right.at[0], rbuf.at[0, pl.ds(pl.multiple_of(r * rows, rows), rows)], local.at[2])

    @pl.when(outer)
    def _():
        r_end().start()

    @pl.when(inner)
    def _():
        copy_g.start()
        copy_r.start()
        r_own().start()

    for d in (1, 2, 3):
        @pl.when(c - d >= 0)
        def _():
            k = c - d
            lz(k, 1, lbuf.at[k, mine]).wait_recv()

            @pl.when(c < 3)
            def _():
                lz(k, 1, lbuf.at[k, mine]).start()
            for t in range(3):
                lxy(k, t).start()

        @pl.when(c + d <= 3)
        def _():
            k = c + d
            lz(k, 0, lbuf.at[k, mine]).wait_recv()

            @pl.when(c > 0)
            def _():
                lz(k, 0, lbuf.at[k, mine]).start()
            for t in range(3):
                lxy(k, t).start()

        if d == 1:
            @pl.when(inner)
            def _():
                g_own().start()

    def chunk(i):
        return pl.ds(i * step if isinstance(i, int) else pl.multiple_of(i * step, step), step)

    def deep(half, i):
        return pl.ds(pl.multiple_of(half * rows + i * step, step), step)

    def near(i):
        return remote(grad.at[0, chunk(i)], gbuf.at[c, chunk(i)], near_send.at[i], near_recv.at[i], (q, r, pair))

    def far(i):
        part = gbuf.at[pair, chunk(i)]
        return remote(part, part, far_send.at[i], far_recv.at[i], (q, r, other))

    def mix_twin(i):
        part = mix.at[deep(r, i)]
        return remote(part, part, ms_send.at[i], ms_recv.at[i], twin)

    def mix_end(i):
        return remote(stage.at[i % 2], mix.at[deep(r, i)], me_send.at[i], me_recv.at[i], (q, r, pair))

    @pl.when(outer)
    def _():
        r_end().wait_send()
        for i in range(CHUNKS):
            near(i).start()
            if i >= 1:
                near(i - 1).wait_send()
        near(CHUNKS - 1).wait_send()
        for i in range(CHUNKS):
            mix_end(i).wait_recv()
            mix_twin(i).start()

    @pl.when(inner)
    def _():
        r_end().wait_recv()
        r_twin().start()
        near(0).wait_recv()
        far(0).start()
        copy_g.wait()
        copy_r.wait()
        r_own().wait_recv()
        g_own().wait_recv()
        r_twin().wait_recv()

        def body(i, _):
            @pl.when(i + 1 < CHUNKS)
            def _():
                near(i + 1).wait_recv()
                far(i + 1).start()
            far(i).wait_recv()

            @pl.when(i >= 2)
            def _():
                mix_end(i - 2).wait_send()

            def tile(n, _, which):
                at = pl.ds(pl.multiple_of(n * 256, 256), 256)
                total = jnp.zeros((step, 256), jnp.float32)
                for k in range(4):
                    total += jnp.dot(
                        gbuf[k, chunk(i), :], rbuf[which, k * cols:(k + 1) * cols, at],
                        preferred_element_type=jnp.float32)
                if which:
                    stage[i % 2, :, at] = total.astype(jnp.bfloat16)
                else:
                    mix[deep(r, i), at] = total.astype(jnp.bfloat16)
                return 0

            lax.fori_loop(0, cols // 256, functools.partial(tile, which=1), 0)
            mix_end(i).start()
            lax.fori_loop(0, cols // 256, functools.partial(tile, which=0), 0)
            mix_twin(i).start()
            return 0

        lax.fori_loop(0, CHUNKS, body, 0)
        mix_end(CHUNKS - 2).wait_send()
        mix_end(CHUNKS - 1).wait_send()
        for i in range(CHUNKS):
            far(i).wait_send()
        r_twin().wait_send()
        r_own().wait_send()
        g_own().wait_send()

    copy_w = pltpu.make_async_copy(wts.at[0], rbuf.at[1, pl.ds(0, rows)], local.at[3])
    copy_w.start()

    order = [(p, h) for p in peers + [q] for h in range(PARTS)]
    size = lane // PARTS

    def strip(t):
        p, h = order[t]
        return pl.ds(pl.multiple_of(p * lane + h * size, size), size)

    def m_load(t):
        return pltpu.make_async_copy(mom.at[0, strip(t)], mslot.at[t % 4], m_in.at[t % 4])

    def m_store(t):
        return pltpu.make_async_copy(mslot.at[t % 4], out_m.at[0, strip(t)], m_out.at[t % 4])

    def spread(t):
        p, h = order[t]
        target = out_w.at[q, pl.ds(h * size, size)]
        source = rbuf.at[1, strip(t)]
        if t // PARTS == 3:
            return pltpu.make_async_copy(source, target, a_send.at[t])
        return remote(source, target, a_send.at[t], a_recv.at[t], (p, r, c))

    m_load(0).start()
    m_load(1).start()
    copy_l.wait()
    for d in (1, 2, 3):
        k = (c + d) % 4
        for p in peers:
            theirs = lbuf.at[k, pl.ds(pl.multiple_of(p * lane, lane), lane)]
            remote(theirs, theirs, lxy_send.at[0], lxy_recv.at[k * 4 + p], twin).wait_recv()
    for i in range(CHUNKS):
        part = mix.at[deep(1 - r, i)]
        remote(part, part, ms_send.at[i], ms_recv.at[i], twin).wait_recv()
    copy_w.wait()

    for t in range(4 * PARTS):
        m_load(t).wait()

        def tile(n, _):
            at = pl.ds(pl.multiple_of(n * 256, 256), 256)
            total = jnp.zeros((size, 256), jnp.float32)
            for k in range(4):
                total += jnp.dot(
                    lbuf[k, strip(t), :], mix[k * cols:(k + 1) * cols, at],
                    preferred_element_type=jnp.float32)
            renewed = decay_rate * mslot[t % 4, :, at] + (1.0 - decay_rate) * total
            mslot[t % 4, :, at] = renewed
            old = rbuf[1, strip(t), at].astype(jnp.float32)
            rbuf[1, strip(t), at] = (old - step_rate * renewed).astype(jnp.bfloat16)
            return 0

        lax.fori_loop(0, cols // 256, tile, 0)
        m_store(t).start()
        spread(t).start()
        if t >= 2:
            m_store(t - 2).wait()
        if t + 2 < 4 * PARTS:
            m_load(t + 2).start()

    m_store(4 * PARTS - 2).wait()
    m_store(4 * PARTS - 1).wait()

    @pl.when(c < 3)
    def _():
        lz(c, 1, left.at[mine]).wait_send()

    @pl.when(c > 0)
    def _():
        lz(c, 0, left.at[mine]).wait_send()

    for d in (1, 2, 3):
        @pl.when(c - d >= 0)
        def _():
            k = c - d

            @pl.when(c < 3)
            def _():
                lz(k, 1, lbuf.at[k, mine]).wait_send()
            for t in range(3):
                lxy(k, t).wait_send()

        @pl.when(c + d <= 3)
        def _():
            k = c + d

            @pl.when(c > 0)
            def _():
                lz(k, 0, lbuf.at[k, mine]).wait_send()
            for t in range(3):
                lxy(k, t).wait_send()

    for i in range(CHUNKS):
        mix_twin(i).wait_send()
    for t in range(3 * PARTS):
        p, h = order[t]
        spread(t).wait_send()
        theirs = out_w.at[p, pl.ds(h * size, size)]
        remote(theirs, theirs, a_send.at[t], a_recv.at[t], (p, r, c)).wait_recv()
    for t in range(3 * PARTS, 4 * PARTS):
        spread(t).wait()


def one_kernel(grad, left_root, right_root, momentum, weights):
    rows, cols = left_root.shape
    bf16, dma = jnp.bfloat16, pltpu.SemaphoreType.DMA
    anywhere = pl.BlockSpec(memory_space=pl.ANY)
    return pl.pallas_call(
        kernel,
        out_shape=(
            jax.ShapeDtypeStruct((1, rows, cols), jnp.float32),
            jax.ShapeDtypeStruct((4, rows // 4, cols), bf16),
        ),
        in_specs=[anywhere] * 5,
        out_specs=(anywhere, anywhere),
        scratch_shapes=[
            pltpu.VMEM((4, rows, cols), bf16),
            pltpu.VMEM((4, rows, cols), bf16),
            pltpu.VMEM((2, 2 * rows, cols), bf16),
            pltpu.VMEM((2 * rows, cols), bf16),
            pltpu.VMEM((2, rows // CHUNKS, cols), bf16),
            pltpu.VMEM((4, rows // 4 // PARTS, cols), jnp.float32),
            dma((8,)), dma((4,)), dma((12,)), dma((16,)), dma((4,)), dma((4,)), dma((4,)),
            dma((CHUNKS,)), dma((CHUNKS,)), dma((CHUNKS,)), dma((CHUNKS,)),
            dma((CHUNKS,)), dma((CHUNKS,)), dma((CHUNKS,)), dma((CHUNKS,)),
            dma((4 * PARTS,)), dma((4 * PARTS,)), dma((4,)), dma((4,)),
        ],
        compiler_params=pltpu.CompilerParams(
            collective_id=0, has_side_effects=True, vmem_limit_bytes=63 * 1024 * 1024),
        cost_estimate=pl.CostEstimate(
            flops=4 * 4 * rows * rows * cols, bytes_accessed=36 * rows * cols, transcendentals=0),
    )(grad, left_root, right_root, momentum, weights)


def by_collectives(grad, left_root, right_root, momentum, weights):
    right_panel = lax.all_gather(right_root, "row", axis=1, tiled=True)[0]
    mixed = jnp.dot(
        lax.all_gather(grad, "col", axis=2, tiled=True)[0],
        right_panel,
        preferred_element_type=jnp.float32,
    ).astype(jnp.bfloat16)
    left_panel = lax.all_gather(left_root, "col", axis=1, tiled=True)
    product = jnp.dot(
        left_panel,
        lax.all_gather(mixed, "row", axis=0, tiled=True),
        preferred_element_type=jnp.float32,
    )
    renewed = decay_rate * momentum[0] + (1.0 - decay_rate) * product
    updated = (weights[0].astype(jnp.float32) - step_rate * renewed).astype(jnp.bfloat16)
    spread = lax.all_to_all(updated[None], "quarter", split_axis=1, concat_axis=0, tiled=True)
    return (renewed[None], spread)


def solution(mesh):
    placed = (
        P("quarter", "row", "col"),
        P("row", "col"),
        P("quarter", "row", "col"),
        P("quarter", "row", "col"),
        P("quarter", "row", "col"),
    )
    shape = mesh.shape
    lines = (shape["quarter"], shape["row"], shape["col"]) == (4, 2, 4)
    return jax.shard_map(
        one_kernel if lines else by_collectives,
        mesh=mesh,
        in_specs=placed,
        out_specs=(P("quarter", "row", "col"), P(None, ("row", "quarter"), "col")),
        check_vma=False,
    )
```

```python
import functools

import jax
import jax.numpy as jnp
from jax import lax
from jax.experimental import pallas as pl
from jax.experimental.pallas import tpu as pltpu
from jax.sharding import PartitionSpec as P

decay_rate = 0.9
step_rate = 0.1

CHUNKS = 8
PARTS = 2


def remote(src, dst, send, recv, device):
    return pltpu.make_async_remote_copy(
        src_ref=src, dst_ref=dst, send_sem=send, recv_sem=recv,
        device_id=device, device_id_type=pl.DeviceIdType.MESH,
    )


def kernel(
    grad, left, right, mom, wts, out_m, out_w,
    lbuf, gbuf, rbuf, mix, stage, mslot,
    lz_send, lz_recv, lxy_send, lxy_recv, local, own_send, own_recv,
    near_send, near_recv, far_send, far_recv,
    ms_send, ms_recv, me_send, me_recv,
    a_send, a_recv, m_in, m_out,
):
    rows, cols = left.shape
    lane = rows // 4
    step = rows // CHUNKS
    q, r, c = lax.axis_index("quarter"), lax.axis_index("row"), lax.axis_index("col")
    peers = [3 - q, q + 1 - 2 * (q % 2), (q + 2) % 4]
    twin = (q, 1 - r, c)
    inner = (c + 1) // 2 % 2 == 1
    outer = (c + 1) // 2 % 2 == 0
    before, after = (q, r, c - 1), (q, r, c + 1)
    low = c // 2 == 0
    pair = c + 1 - 2 * (c % 2)
    other = 3 - c
    mine = pl.ds(pl.multiple_of(q * lane, lane), lane)

    barrier = pltpu.get_barrier_semaphore()
    for p in peers:
        pl.semaphore_signal(barrier, inc=1, device_id=(p, r, c), device_id_type=pl.DeviceIdType.MESH)
    pl.semaphore_signal(barrier, inc=1, device_id=twin, device_id_type=pl.DeviceIdType.MESH)

    @pl.when(c > 0)
    def _():
        pl.semaphore_signal(barrier, inc=1, device_id=before, device_id_type=pl.DeviceIdType.MESH)

    @pl.when(c < 3)
    def _():
        pl.semaphore_signal(barrier, inc=1, device_id=after, device_id_type=pl.DeviceIdType.MESH)

    @pl.when(inner)
    def _():
        pl.semaphore_wait(barrier, 6)

    @pl.when(outer)
    def _():
        pl.semaphore_wait(barrier, 5)

    def lz(k, way, src):
        return remote(src, lbuf.at[k, mine], lz_send.at[k * 2 + way], lz_recv.at[k], after if way else before)

    def lxy(k, t):
        piece = lbuf.at[k, mine]
        return remote(piece, piece, lxy_send.at[k * 3 + t], lxy_recv.at[k * 4 + q], (peers[t], r, c))

    @pl.when(c < 3)
    def _():
        lz(c, 1, left.at[mine]).start()

    @pl.when(c > 0)
    def _():
        lz(c, 0, left.at[mine]).start()

    copy_l = pltpu.make_async_copy(left, lbuf.at[c], local.at[0])
    copy_l.start()

    def g_own():
        return remote(grad.at[0], gbuf.at[c], own_send.at[0], own_recv.at[0], (q, r, other))

    def r_own():
        half = rbuf.at[0, pl.ds(pl.multiple_of(r * rows, rows), rows)]
        return remote(right.at[0], half, own_send.at[1], own_recv.at[1], twin)

    def r_end():
        half = rbuf.at[1, pl.ds(pl.multiple_of(r * rows, rows), rows)]
        return remote(right.at[0], half, own_send.at[2], own_recv.at[2], (q, r, pair))

    def r_twin():
        half = rbuf.at[1, pl.ds(pl.multiple_of(r * rows, rows), rows)]
        return remote(half, half, own_send.at[3], own_recv.at[3], twin)

    copy_g = pltpu.make_async_copy(grad.at[0], gbuf.at[c], local.at[1])
    copy_r = pltpu.make_async_copy(
        right.at[0], rbuf.at[0, pl.ds(pl.multiple_of(r * rows, rows), rows)], local.at[2])

    @pl.when(outer)
    def _():
        @pl.when(c == 0)
        def _():
            lz(c, 1, left.at[mine]).wait_send()

        @pl.when(c == 3)
        def _():
            lz(c, 0, left.at[mine]).wait_send()
        r_end().start()

    @pl.when(inner)
    def _():
        copy_g.start()
        copy_r.start()
        r_own().start()

    for d in (1, 2, 3):
        @pl.when(c - d >= 0)
        def _():
            k = c - d
            lz(k, 1, lbuf.at[k, mine]).wait_recv()

            @pl.when(c < 3)
            def _():
                lz(k, 1, lbuf.at[k, mine]).start()
            for t in range(3):
                lxy(k, t).start()

        @pl.when(c + d <= 3)
        def _():
            k = c + d
            lz(k, 0, lbuf.at[k, mine]).wait_recv()

            @pl.when(c > 0)
            def _():
                lz(k, 0, lbuf.at[k, mine]).start()
            for t in range(3):
                lxy(k, t).start()

        if d == 2:
            @pl.when(inner)
            def _():
                g_own().start()

    def chunk(i):
        return pl.ds(i * step if isinstance(i, int) else pl.multiple_of(i * step, step), step)

    def deep(half, i):
        return pl.ds(pl.multiple_of(half * rows + i * step, step), step)

    def near(i):
        return remote(grad.at[0, chunk(i)], gbuf.at[c, chunk(i)], near_send.at[i], near_recv.at[i], (q, r, pair))

    def far(i):
        part = gbuf.at[pair, chunk(i)]
        return remote(part, part, far_send.at[i], far_recv.at[i], (q, r, other))

    def mix_twin(i):
        part = mix.at[deep(r, i)]
        return remote(part, part, ms_send.at[i], ms_recv.at[i], twin)

    def mix_end(i):
        return remote(stage.at[i % 2], mix.at[deep(r, i)], me_send.at[i], me_recv.at[i], (q, r, pair))

    @pl.when(outer)
    def _():
        r_end().wait_send()
        for i in range(CHUNKS):
            near(i).start()
            if i >= 1:
                near(i - 1).wait_send()
        near(CHUNKS - 1).wait_send()
        for i in range(CHUNKS):
            mix_end(i).wait_recv()
            mix_twin(i).start()

    @pl.when(inner)
    def _():
        r_end().wait_recv()
        r_twin().start()
        near(0).wait_recv()
        far(0).start()
        copy_g.wait()
        copy_r.wait()
        r_own().wait_recv()
        g_own().wait_recv()
        r_twin().wait_recv()

        def body(i, _):
            @pl.when(i + 1 < CHUNKS)
            def _():
                near(i + 1).wait_recv()
                far(i + 1).start()
            far(i).wait_recv()

            @pl.when(i >= 2)
            def _():
                mix_end(i - 2).wait_send()

            def tile(n, _, which):
                at = pl.ds(pl.multiple_of(n * 256, 256), 256)
                total = jnp.zeros((step, 256), jnp.float32)
                for k in range(4):
                    total += jnp.dot(
                        gbuf[k, chunk(i), :], rbuf[which, k * cols:(k + 1) * cols, at],
                        preferred_element_type=jnp.float32)
                if which:
                    stage[i % 2, :, at] = total.astype(jnp.bfloat16)
                else:
                    mix[deep(r, i), at] = total.astype(jnp.bfloat16)
                return 0

            lax.fori_loop(0, cols // 256, functools.partial(tile, which=1), 0)
            mix_end(i).start()
            lax.fori_loop(0, cols // 256, functools.partial(tile, which=0), 0)
            mix_twin(i).start()
            return 0

        lax.fori_loop(0, CHUNKS, body, 0)
        mix_end(CHUNKS - 2).wait_send()
        mix_end(CHUNKS - 1).wait_send()
        for i in range(CHUNKS):
            far(i).wait_send()
        r_twin().wait_send()
        r_own().wait_send()
        g_own().wait_send()

    copy_w = pltpu.make_async_copy(wts.at[0], rbuf.at[1, pl.ds(0, rows)], local.at[3])
    copy_w.start()

    order = [(p, h) for p in peers + [q] for h in range(PARTS)]
    size = lane // PARTS

    def strip(t):
        p, h = order[t]
        return pl.ds(pl.multiple_of(p * lane + h * size, size), size)

    def m_load(t):
        return pltpu.make_async_copy(mom.at[0, strip(t)], mslot.at[t % 4], m_in.at[t % 4])

    def m_store(t):
        return pltpu.make_async_copy(mslot.at[t % 4], out_m.at[0, strip(t)], m_out.at[t % 4])

    def spread(t):
        p, h = order[t]
        target = out_w.at[q, pl.ds(h * size, size)]
        source = rbuf.at[1, strip(t)]
        if t // PARTS == 3:
            return pltpu.make_async_copy(source, target, a_send.at[t])
        return remote(source, target, a_send.at[t], a_recv.at[t], (p, r, c))

    m_load(0).start()
    m_load(1).start()
    copy_l.wait()
    for d in (1, 2, 3):
        k = (c + d) % 4
        for p in peers:
            theirs = lbuf.at[k, pl.ds(pl.multiple_of(p * lane, lane), lane)]
            remote(theirs, theirs, lxy_send.at[0], lxy_recv.at[k * 4 + p], twin).wait_recv()
    for i in range(CHUNKS):
        part = mix.at[deep(1 - r, i)]
        remote(part, part, ms_send.at[i], ms_recv.at[i], twin).wait_recv()
    copy_w.wait()

    for t in range(4 * PARTS):
        m_load(t).wait()

        def tile(n, _):
            at = pl.ds(pl.multiple_of(n * 256, 256), 256)
            total = jnp.zeros((size, 256), jnp.float32)
            for k in range(4):
                total += jnp.dot(
                    lbuf[k, strip(t), :], mix[k * cols:(k + 1) * cols, at],
                    preferred_element_type=jnp.float32)
            renewed = decay_rate * mslot[t % 4, :, at] + (1.0 - decay_rate) * total
            mslot[t % 4, :, at] = renewed
            old = rbuf[1, strip(t), at].astype(jnp.float32)
            rbuf[1, strip(t), at] = (old - step_rate * renewed).astype(jnp.bfloat16)
            return 0

        lax.fori_loop(0, cols // 256, tile, 0)
        m_store(t).start()
        spread(t).start()
        if t >= 2:
            m_store(t - 2).wait()
        if t + 2 < 4 * PARTS:
            m_load(t + 2).start()

    m_store(4 * PARTS - 2).wait()
    m_store(4 * PARTS - 1).wait()

    @pl.when(inner)
    def _():
        lz(c, 1, left.at[mine]).wait_send()
        lz(c, 0, left.at[mine]).wait_send()

    for d in (1, 2, 3):
        @pl.when(c - d >= 0)
        def _():
            k = c - d

            @pl.when(c < 3)
            def _():
                lz(k, 1, lbuf.at[k, mine]).wait_send()
            for t in range(3):
                lxy(k, t).wait_send()

        @pl.when(c + d <= 3)
        def _():
            k = c + d

            @pl.when(c > 0)
            def _():
                lz(k, 0, lbuf.at[k, mine]).wait_send()
            for t in range(3):
                lxy(k, t).wait_send()

    for i in range(CHUNKS):
        mix_twin(i).wait_send()
    for t in range(3 * PARTS):
        p, h = order[t]
        spread(t).wait_send()
        theirs = out_w.at[p, pl.ds(h * size, size)]
        remote(theirs, theirs, a_send.at[t], a_recv.at[t], (p, r, c)).wait_recv()
    for t in range(3 * PARTS, 4 * PARTS):
        spread(t).wait()


def one_kernel(grad, left_root, right_root, momentum, weights):
    rows, cols = left_root.shape
    bf16, dma = jnp.bfloat16, pltpu.SemaphoreType.DMA
    anywhere = pl.BlockSpec(memory_space=pl.ANY)
    return pl.pallas_call(
        kernel,
        out_shape=(
            jax.ShapeDtypeStruct((1, rows, cols), jnp.float32),
            jax.ShapeDtypeStruct((4, rows // 4, cols), bf16),
        ),
        in_specs=[anywhere] * 5,
        out_specs=(anywhere, anywhere),
        scratch_shapes=[
            pltpu.VMEM((4, rows, cols), bf16),
            pltpu.VMEM((4, rows, cols), bf16),
            pltpu.VMEM((2, 2 * rows, cols), bf16),
            pltpu.VMEM((2 * rows, cols), bf16),
            pltpu.VMEM((2, rows // CHUNKS, cols), bf16),
            pltpu.VMEM((4, rows // 4 // PARTS, cols), jnp.float32),
            dma((8,)), dma((4,)), dma((12,)), dma((16,)), dma((4,)), dma((4,)), dma((4,)),
            dma((CHUNKS,)), dma((CHUNKS,)), dma((CHUNKS,)), dma((CHUNKS,)),
            dma((CHUNKS,)), dma((CHUNKS,)), dma((CHUNKS,)), dma((CHUNKS,)),
            dma((4 * PARTS,)), dma((4 * PARTS,)), dma((4,)), dma((4,)),
        ],
        compiler_params=pltpu.CompilerParams(
            collective_id=0, has_side_effects=True, vmem_limit_bytes=63 * 1024 * 1024),
        cost_estimate=pl.CostEstimate(
            flops=4 * 4 * rows * rows * cols, bytes_accessed=36 * rows * cols, transcendentals=0),
    )(grad, left_root, right_root, momentum, weights)


def by_collectives(grad, left_root, right_root, momentum, weights):
    right_panel = lax.all_gather(right_root, "row", axis=1, tiled=True)[0]
    mixed = jnp.dot(
        lax.all_gather(grad, "col", axis=2, tiled=True)[0],
        right_panel,
        preferred_element_type=jnp.float32,
    ).astype(jnp.bfloat16)
    left_panel = lax.all_gather(left_root, "col", axis=1, tiled=True)
    product = jnp.dot(
        left_panel,
        lax.all_gather(mixed, "row", axis=0, tiled=True),
        preferred_element_type=jnp.float32,
    )
    renewed = decay_rate * momentum[0] + (1.0 - decay_rate) * product
    updated = (weights[0].astype(jnp.float32) - step_rate * renewed).astype(jnp.bfloat16)
    spread = lax.all_to_all(updated[None], "quarter", split_axis=1, concat_axis=0, tiled=True)
    return (renewed[None], spread)


def solution(mesh):
    placed = (
        P("quarter", "row", "col"),
        P("row", "col"),
        P("quarter", "row", "col"),
        P("quarter", "row", "col"),
        P("quarter", "row", "col"),
    )
    shape = mesh.shape
    lines = (shape["quarter"], shape["row"], shape["col"]) == (4, 2, 4)
    return jax.shard_map(
        one_kernel if lines else by_collectives,
        mesh=mesh,
        in_specs=placed,
        out_specs=(P("quarter", "row", "col"), P(None, ("row", "quarter"), "col")),
        check_vma=False,
    )
```
